32 devices in a mesh: parts: 1, sec: 32 (over z, y, x, core).
Axes of the slice: x: 2, y: 2, z: 4, core: 2. Of those that a mesh axis runs over, the one named last changes fastest.
Arguments:
- queries: bfloat16 [8192, 1024], P(('parts', 'sec')), may hold values from -6 to 6
- keys: bfloat16 [8192, 1024], P(('parts', 'sec')), may hold values from -6 to 6
- values: bfloat16 [8192, 2048], P(('parts', 'sec')), may hold values from -6 to 6
- gate_codes: int32 [8192, 16], P(('parts', 'sec')), may hold values from 0 to 5734
- beta_codes: int32 [8192, 16], P(('parts', 'sec')), may hold values from 16 to 4096
- norm_gain: float32 [128], replicated, may hold values from 0.5 to 1.5
Outputs:
- head_out: bfloat16 [8192, 2048], P(('parts', 'sec'))
- final_state: float32 [2048, 128], P(('parts', 'sec'))
The draws below stay inside these ranges and needn't reach their ends.
All inputs are finite; a program needn't handle non-finite values.
Results may differ from the reference program's by a relative error of at most 0.001.
Values sent between devices are 32-bit elements; how exact they have to be, the bound alone decides.
A program may use at most 320 MiB of HBM per device.

```python
import jax
import jax.numpy as jnp
from jax import lax

DK = 128
DV = 128
VH = 16
KH = 8
TOK_DEV = 256
TOKENS = 8192


def quick_heads(key):
    order = jax.random.permutation(jax.random.fold_in(key, 7), VH)
    quick_count = jax.random.randint(jax.random.fold_in(key, 6), (), 0, VH // 2 + 1)
    return order < quick_count


def draw_gate_codes(key, part):
    quick = quick_heads(key)
    slow_codes = jax.random.randint(jax.random.fold_in(key, 11), (TOKENS, VH), 0, 2)
    section_factor = 1 + jax.random.randint(jax.random.fold_in(key, 12), (TOKENS // TOK_DEV, VH), 0, 2)
    section_ids = jnp.arange(TOKENS) // TOK_DEV
    slow_codes = slow_codes * jnp.take(section_factor, section_ids, axis=0)
    fast_codes = jax.random.randint(jax.random.fold_in(key, 13), (TOKENS, VH), TOKENS // 60, TOKENS // 30 + 1)
    random_labels = jnp.where(quick[None, :], fast_codes, slow_codes)
    section_positions = jax.random.randint(jax.random.fold_in(key, 14), (2, VH), 0, TOKENS)
    decay_levels = jax.random.randint(jax.random.fold_in(key, 15), (2, VH), TOKENS // 5, 7 * TOKENS // 10 + 1)
    decay_levels = decay_levels.at[0].set(7 * TOKENS // 10)
    row_index = jnp.arange(TOKENS)[:, None]
    for section_tokens in range(2):
        random_labels = jnp.where(row_index == section_positions[section_tokens][None, :], jnp.maximum(random_labels, decay_levels[section_tokens][None, :]), random_labels)
    return random_labels.astype(jnp.int32)


def draw_beta_codes(key, part):
    quick = quick_heads(key)
    slow_codes = jax.random.randint(jax.random.fold_in(key, 21), (TOKENS, VH), 16, 49)
    fast_codes = jax.random.randint(jax.random.fold_in(key, 22), (TOKENS, VH), TOKENS // 4, TOKENS // 2 + 1)
    random_labels = jnp.where(quick[None, :], fast_codes, slow_codes)
    random_labels = random_labels.at[0].set(jnp.full((VH,), TOKENS // 2, dtype=random_labels.dtype))
    return random_labels.astype(jnp.int32)


def steps_of(key, dims, shards, least, largest):
    def one(axis_at, shards_of):
        heights = jax.random.uniform(jax.random.fold_in(jax.random.fold_in(key, 6), axis_at), (shards_of,), jnp.float32, least / len(shards), largest / len(shards))
        return jnp.repeat(jnp.exp(heights), dims[axis_at] // shards_of).reshape((-1,) + (1,) * (len(dims) - axis_at - 1))

    factor_of = one(*shards[0])
    for cut in shards[1:]:
        factor_of = factor_of * one(*cut)
    return factor_of


def scatter_about(own_key, shape, deviation, bound, shards=(), held_as=jnp.bfloat16):
    values = jax.random.normal(own_key, shape, jnp.float32) * deviation
    if len(shards) > 0:
        values = steps_of(own_key, shape, shards, -0.22, 0.18) * values
    return jnp.clip(values, min=-bound, max=bound).astype(held_as)


def setup_inputs(seed: int = 0, part: int = 0) -> dict:
    key_of = jax.random.split(jax.random.key(seed), 7)
    own_keys = jax.random.split(jax.random.fold_in(key_of[6], part), 7)
    queries = scatter_about(own_keys[0], (TOKENS, KH * DK), 1.0, 6.0, ((0, 32),))
    keys = scatter_about(own_keys[1], (TOKENS, KH * DK), 1.0, 6.0, ((0, 32),))
    values = scatter_about(own_keys[2], (TOKENS, VH * DV), 1.0, 6.0, ((0, 32),))
    gate_codes = draw_gate_codes(jax.random.fold_in(jax.random.fold_in(key_of[6], part), 71), part)
    beta_codes = draw_beta_codes(jax.random.fold_in(jax.random.fold_in(key_of[6], part), 71), part)
    norm_gain = jnp.clip(1.0 + 0.1 * jax.random.normal(key_of[5], (DV,), jnp.float32), 0.5, 1.5)
    return {"queries": queries, "keys": keys, "values": values, "gate_codes": gate_codes, "beta_codes": beta_codes, "norm_gain": norm_gain}


def normalize(rows, factor):
    return rows * lax.rsqrt(lax.optimization_barrier(jnp.sum(rows * rows, axis=-1, keepdims=True)) + 1e-06) * factor

def reference(queries, keys, values, gate_codes, beta_codes, norm_gain):
    group = VH // KH
    query_rows = normalize(queries.astype(jnp.float32).reshape(TOKENS, KH, DK), DK ** (-0.5))
    key_matrix = normalize(keys.astype(jnp.float32).reshape(TOKENS, KH, DK), 1.0)
    query_rows = jnp.repeat(query_rows, group, axis=1)
    key_matrix = jnp.repeat(key_matrix, group, axis=1)
    value_rows = values.astype(jnp.float32).reshape(TOKENS, VH, DV)
    decay_factor = jnp.exp(-gate_codes.astype(jnp.float32) / TOKENS)
    beta_rows = beta_codes.astype(jnp.float32) / TOKENS

    def advance(state_matrix, inputs):
        step_query, step_key, value_t, decay_t, beta_t = inputs
        state_matrix = decay_t[:, None, None] * state_matrix
        retrieved_value = jnp.einsum('iy,iyn->in', step_key, state_matrix, precision=lax.Precision.HIGHEST)
        state_matrix = state_matrix + beta_t[:, None, None] * step_key[:, :, None] * (value_t - retrieved_value)[:, None, :]
        step_output = jnp.einsum('iy,iyn->in', step_query, state_matrix, precision=lax.Precision.HIGHEST)
        return (state_matrix, step_output)
    start = jnp.zeros((VH, DK, DV), jnp.float32)
    final_mat, output_rows = lax.scan(advance, start, (query_rows, key_matrix, value_rows, decay_factor, beta_rows))
    scaled = output_rows * lax.rsqrt(lax.optimization_barrier(jnp.mean(output_rows * output_rows, axis=-1, keepdims=True)) + 1e-06) * norm_gain
    head_out = scaled.reshape(TOKENS, VH * DV).astype(jnp.bfloat16)
    return (head_out, final_mat.reshape(VH * DK, DV))
```

```python
import functools

import jax
import jax.numpy as jnp
from jax import lax
from jax.experimental import pallas as pl
from jax.experimental.pallas import tpu as pltpu
from jax.sharding import PartitionSpec as P

DK = 128
HALF = 128
F32 = jnp.float32
BF16 = jnp.bfloat16
ROWS_BY_ROWS = (((1,), (1,)), ((), ()))
DOWN = (((0,), (0,)), ((), ()))
PLAIN = (((1,), (0,)), ((), ()))


def cut(a):
    high = a.astype(BF16)
    return high, (a - high.astype(F32)).astype(BF16)


def dot(left, right, dims=PLAIN):
    return lax.dot_general(left, right, dims, preferred_element_type=F32)


def dot3(left, right, dims=PLAIN):
    lh, ll = cut(left)
    rh, rl = cut(right)
    return dot(lh, rh, dims) + (dot(lh, rl, dims) + dot(ll, rh, dims))


def section_kernel(total, q_ref, k_ref, v_ref, ccol_ref, crow_ref, b_ref, ab_ref, o_ref, p_ref):
    tokens = q_ref.shape[0]
    group = v_ref.shape[1] // DK
    q = q_ref[...]
    k = k_ref[...]
    qf = q.astype(F32)
    kf = k.astype(F32)
    rq = lax.rsqrt(jnp.sum(qf * qf, axis=1, keepdims=True) + 1e-06) * DK ** (-0.5)
    rk = lax.rsqrt(jnp.sum(kf * kf, axis=1, keepdims=True) + 1e-06)
    rk_row = jnp.transpose(jnp.broadcast_to(rk, (tokens, DK)))[0:1, :]
    kk = dot(k, k, ROWS_BY_ROWS) * rk * rk_row
    qk = dot(q, k, ROWS_BY_ROWS) * rq * rk_row
    row = lax.broadcasted_iota(jnp.int32, (tokens, tokens), 0)
    col = lax.broadcasted_iota(jnp.int32, (tokens, tokens), 1)
    r = row[:HALF, :HALF]
    c = col[:HALF, :HALF]
    eye = (r == c).astype(F32)
    blocks = tokens // HALF
    lowers, xs = [], []
    data = []
    for w in range(group):
        ccol = ccol_ref[0, :, w : w + 1]
        crow = crow_ref[0, w : w + 1, :]
        beta = b_ref[0, :, w : w + 1]
        gap = jnp.where(row >= col, (ccol - crow) * (-1.0 / total), -1e30)
        mask = jnp.exp(gap)
        lower = jnp.where(row > col, kk * mask * beta, 0.0)
        grown = jnp.exp(ccol * (-1.0 / total))
        last = ccol[tokens - 1 : tokens, :]
        left = jnp.exp((last - ccol) * (-1.0 / total)) * rk
        final = jnp.exp(last * (-1.0 / total))
        right = jnp.concatenate(
            [kf * (rk * beta * grown), v_ref[:, w * DK : (w + 1) * DK].astype(F32) * beta], axis=1
        )
        data.append((lower, qk * mask, grown, left, final, right))
        for b in range(blocks):
            part = lower[b * HALF : (b + 1) * HALF, b * HALF : (b + 1) * HALF]
            lowers.append(part)
            xs.append(eye - jnp.where((r // 2) == (c // 2), part, 0.0))
    size = 2
    while size < HALF:
        inside = ((r // (2 * size)) == (c // (2 * size))) & ((r // size) != (c // size))
        cuts = [cut(x) for x in xs]
        mids = []
        for part, (xh, xl) in zip(lowers, cuts):
            mh, ml = cut(jnp.where(inside, part, 0.0))
            mids.append(dot(mh, xh) + (dot(mh, xl) + dot(ml, xh)))
        news = []
        for x, (xh, xl), mid in zip(xs, cuts, mids):
            yh, yl = cut(mid)
            news.append(x - (dot(xh, yh) + (dot(xh, yl) + dot(xl, yh))))
        xs = news
        size *= 2
    for w in range(group):
        lower, scores, grown, left, final, right = data[w]
        parts = []
        for b in range(blocks):
            rows = slice(b * HALF, (b + 1) * HALF)
            rhs = right[rows]
            for e in range(b):
                rhs = rhs - dot3(lower[rows, e * HALF : (e + 1) * HALF], parts[e])
            parts.append(dot3(xs[w * blocks + b], rhs))
        solved = jnp.concatenate(parts, axis=0)
        read = dot3(scores, solved)
        o_ref[w] = read[:, DK:]
        p_ref[w] = qf * (rq * grown) - read[:, :DK]
        sh, sl = cut(solved * left)
        moved = dot(k, sh, DOWN) + dot(k, sl, DOWN)
        ab_ref[w, :, :DK] = final * eye - moved[:, :DK]
        ab_ref[w, :, DK:] = moved[:, DK:]


def section(total, queries, keys, values, codes, beta):
    tokens, heads = codes.shape
    key_heads = queries.shape[1] // DK
    group = heads // key_heads
    sums = jnp.cumsum(codes, axis=0).astype(F32).reshape(tokens, key_heads, group)
    beta = (beta.astype(F32) / total).reshape(tokens, key_heads, group)
    col = lambda h: (0, h)
    lead = lambda h: (h, 0, 0)
    return pl.pallas_call(
        functools.partial(section_kernel, total),
        grid=(key_heads,),
        in_specs=[
            pl.BlockSpec((tokens, DK), col),
            pl.BlockSpec((tokens, DK), col),
            pl.BlockSpec((tokens, group * DK), col),
            pl.BlockSpec((1, tokens, group), lead),
            pl.BlockSpec((1, group, tokens), lead),
            pl.BlockSpec((1, tokens, group), lead),
        ],
        out_specs=[
            pl.BlockSpec((group, DK, 2 * DK), lead),
            pl.BlockSpec((group, tokens, DK), lead),
            pl.BlockSpec((group, tokens, DK), lead),
        ],
        out_shape=[
            jax.ShapeDtypeStruct((heads, DK, 2 * DK), F32),
            jax.ShapeDtypeStruct((heads, tokens, DK), F32),
            jax.ShapeDtypeStruct((heads, tokens, DK), F32),
        ],
        compiler_params=pltpu.CompilerParams(vmem_limit_bytes=40 * 1024 * 1024),
        name="section",
    )(
        queries,
        keys,
        values,
        jnp.transpose(sums, (1, 0, 2)),
        jnp.transpose(sums, (1, 2, 0)),
        jnp.transpose(beta, (1, 0, 2)),
    )


def total_kernel(ab_ref, out_ref):
    sections, heads = ab_ref.shape[:2]
    for h in range(heads):
        out_ref[h] = ab_ref[0, h]
    for s in range(1, sections):
        for h in range(heads):
            new = dot3(ab_ref[s, h, :, :DK], out_ref[h])
            out_ref[h, :, :DK] = new[:, :DK]
            out_ref[h, :, DK:] = new[:, DK:] + ab_ref[s, h, :, DK:]


def total_map(ab):
    return pl.pallas_call(
        total_kernel,
        out_shape=jax.ShapeDtypeStruct(ab.shape[1:], F32),
        compiler_params=pltpu.CompilerParams(vmem_limit_bytes=40 * 1024 * 1024),
        name="total",
    )(ab)


def enter_kernel(place_ref, ab_ref, all_ref, enter_ref, final_ref):
    sections, heads = ab_ref.shape[:2]
    planes = all_ref.shape[0]
    place = place_ref[0]
    for h in range(heads):
        state = jnp.zeros((DK, DK), F32)
        mine = state
        for z in range(planes):
            mine = jnp.where(place == z, state, mine)
            later = all_ref[z, h, :, DK:]
            state = later if z == 0 else dot3(all_ref[z, h, :, :DK], state) + later
        final_ref[h] = state
        enter_ref[0, h] = mine
    for s in range(1, sections):
        for h in range(heads):
            enter_ref[s, h] = (
                dot3(ab_ref[s - 1, h, :, :DK], enter_ref[s - 1, h]) + ab_ref[s - 1, h, :, DK:]
            )


def enter(place, ab, every):
    sections, heads = ab.shape[:2]
    vmem = pl.BlockSpec(memory_space=pltpu.VMEM)
    return pl.pallas_call(
        enter_kernel,
        in_specs=[pl.BlockSpec(memory_space=pltpu.SMEM), vmem, vmem],
        out_specs=[vmem, vmem],
        out_shape=[
            jax.ShapeDtypeStruct((sections, heads, DK, DK), F32),
            jax.ShapeDtypeStruct((heads, DK, DK), F32),
        ],
        compiler_params=pltpu.CompilerParams(vmem_limit_bytes=40 * 1024 * 1024),
        name="enter",
    )(place, ab, every)


def output_kernel(o_ref, p_ref, s_ref, gain_ref, out_ref):
    for w in range(o_ref.shape[0]):
        o = o_ref[w] + dot3(p_ref[w], s_ref[w])
        scale = lax.rsqrt(jnp.mean(o * o, axis=1, keepdims=True) + 1e-06)
        out_ref[:, w * DK : (w + 1) * DK] = (o * scale * gain_ref[...]).astype(BF16)


def output(own, reach, state, gain, group):
    heads, tokens, _ = own.shape
    lead = lambda h: (h, 0, 0)
    return pl.pallas_call(
        output_kernel,
        grid=(heads // group,),
        in_specs=[
            pl.BlockSpec((group, tokens, DK), lead),
            pl.BlockSpec((group, tokens, DK), lead),
            pl.BlockSpec((group, DK, DK), lead),
            pl.BlockSpec((1, DK), lambda h: (0, 0)),
        ],
        out_specs=pl.BlockSpec((tokens, group * DK), lambda h: (0, h)),
        out_shape=jax.ShapeDtypeStruct((tokens, heads * DK), BF16),
        compiler_params=pltpu.CompilerParams(vmem_limit_bytes=40 * 1024 * 1024),
        name="output",
    )(own, reach, state, gain.reshape(1, DK))


def shards(queries, keys, values, gate_codes, beta_codes, norm_gain):
    tokens, heads = gate_codes.shape
    sections = lax.axis_size("sec")
    place = lax.axis_index("sec")
    total = tokens * sections
    plane = 8
    planes = sections // plane
    kept = heads // plane
    ab, own, reach = section(total, queries, keys, values, gate_codes, beta_codes)
    near = [[z * plane + r for r in range(plane)] for z in range(planes)]
    far = [[z * plane + r for z in range(planes)] for r in range(plane)]
    ab = lax.all_to_all(
        ab.reshape(plane, kept, DK, 2 * DK), "sec", 0, 0, axis_index_groups=near, tiled=True
    )
    every = lax.all_gather(total_map(ab), "sec", axis_index_groups=far)
    z, r = place // plane, place % plane
    entering, final = enter(z.reshape(1), ab, every)
    rows = heads * DK // sections
    span = kept * DK
    final = final.reshape(span, DK)
    starts = [(z * plane + d) * rows - r * span for d in range(plane)]
    ends = jnp.stack([lax.dynamic_slice_in_dim(final, jnp.clip(s, 0, span - rows), rows, 0) for s in starts])
    back = lax.all_to_all(
        jnp.concatenate([entering.reshape(plane, span, DK), ends], axis=1),
        "sec", 0, 0, axis_index_groups=near, tiled=True,
    )
    state = back[:, :span].reshape(heads, DK, DK)
    owner = (place * rows) // span
    final_state = lax.dynamic_index_in_dim(back[:, span:], owner, 0, False)
    group = heads // (queries.shape[1] // DK)
    return output(own, reach, state, norm_gain, group), final_state


def solution(mesh):
    rows = P(("parts", "sec"), None)
    return jax.shard_map(
        shards,
        mesh=mesh,
        in_specs=(rows, rows, rows, rows, rows, P()),
        out_specs=(rows, rows),
        check_vma=False,
    )
```

```python
import functools

import jax
import jax.numpy as jnp
from jax import lax
from jax.experimental import pallas as pl
from jax.experimental.pallas import tpu as pltpu
from jax.sharding import PartitionSpec as P

DK = 128
HALF = 128
F32 = jnp.float32
BF16 = jnp.bfloat16
ROWS_BY_ROWS = (((1,), (1,)), ((), ()))
DOWN = (((0,), (0,)), ((), ()))
PLAIN = (((1,), (0,)), ((), ()))


def cut(a):
    high = a.astype(BF16)
    return high, (a - high.astype(F32)).astype(BF16)


def dot(left, right, dims=PLAIN):
    return lax.dot_general(left, right, dims, preferred_element_type=F32)


def dot3(left, right, dims=PLAIN):
    lh, ll = cut(left)
    rh, rl = cut(right)
    return dot(lh, rh, dims) + (dot(lh, rl, dims) + dot(ll, rh, dims))


def section_map(total, h, q_ref, k_ref, v_ref, ccol_ref, crow_ref, b_ref, ab_ref, o_ref, p_ref):
    tokens = q_ref.shape[0]
    key_heads = q_ref.shape[1] // DK
    group = v_ref.shape[1] // DK // key_heads
    q = q_ref[:, pl.ds(pl.multiple_of(h * DK, DK), DK)]
    k = k_ref[:, pl.ds(pl.multiple_of(h * DK, DK), DK)]
    v = v_ref[:, pl.ds(pl.multiple_of(h * group * DK, DK), group * DK)]
    ccols, crows, betas = ccol_ref[h], crow_ref[h], b_ref[h]
    qf = q.astype(F32)
    kf = k.astype(F32)
    rq = lax.rsqrt(jnp.sum(qf * qf, axis=1, keepdims=True) + 1e-06) * DK ** (-0.5)
    rk = lax.rsqrt(jnp.sum(kf * kf, axis=1, keepdims=True) + 1e-06)
    rk_row = jnp.transpose(jnp.broadcast_to(rk, (tokens, DK)))[0:1, :]
    kk = dot(k, k, ROWS_BY_ROWS) * rk * rk_row
    qk = dot(q, k, ROWS_BY_ROWS) * rq * rk_row
    row = lax.broadcasted_iota(jnp.int32, (tokens, tokens), 0)
    col = lax.broadcasted_iota(jnp.int32, (tokens, tokens), 1)
    r = row[:HALF, :HALF]
    c = col[:HALF, :HALF]
    eye = (r == c).astype(F32)
    blocks = tokens // HALF
    lowers, xs, data = [], [], []
    for w in range(group):
        ccol = ccols[:, w : w + 1]
        crow = crows[w : w + 1, :]
        beta = betas[:, w : w + 1]
        gap = jnp.where(row >= col, (ccol - crow) * (-1.0 / total), -1e30)
        mask = jnp.exp(gap)
        lower = jnp.where(row > col, kk * mask * beta, 0.0)
        grown = jnp.exp(ccol * (-1.0 / total))
        last = ccol[tokens - 1 : tokens, :]
        left = jnp.exp((last - ccol) * (-1.0 / total)) * rk
        final = jnp.exp(last * (-1.0 / total))
        right = jnp.concatenate(
            [kf * (rk * beta * grown), v[:, w * DK : (w + 1) * DK].astype(F32) * beta], axis=1
        )
        data.append((lower, qk * mask, grown, left, final, right))
        for b in range(blocks):
            part = lower[b * HALF : (b + 1) * HALF, b * HALF : (b + 1) * HALF]
            lowers.append(part)
            xs.append(eye - jnp.where((r >> 1) == (c >> 1), part, 0.0))
    bit = 1
    while (1 << bit) < HALF:
        inside = ((r >> (bit + 1)) == (c >> (bit + 1))) & ((r >> bit) != (c >> bit))
        cuts = [cut(x) for x in xs]
        mids = []
        for part, (xh, xl) in zip(lowers, cuts):
            mh, ml = cut(jnp.where(inside, part, 0.0))
            mids.append(dot(mh, xh) + (dot(mh, xl) + dot(ml, xh)))
        news = []
        for x, (xh, xl), mid in zip(xs, cuts, mids):
            yh, yl = cut(mid)
            news.append(x - (dot(xh, yh) + (dot(xh, yl) + dot(xl, yh))))
        xs = news
        bit += 1
    for w in range(group):
        lower, scores, grown, left, final, right = data[w]
        parts = []
        for b in range(blocks):
            rows = slice(b * HALF, (b + 1) * HALF)
            rhs = right[rows]
            for e in range(b):
                rhs = rhs - dot3(lower[rows, e * HALF : (e + 1) * HALF], parts[e])
            parts.append(dot3(xs[w * blocks + b], rhs))
        solved = jnp.concatenate(parts, axis=0)
        read = dot3(scores, solved)
        o_ref[h, w] = read[:, DK:]
        p_ref[h, w] = qf * (rq * grown) - read[:, :DK]
        sh, sl = cut(solved * left)
        moved = dot(k, sh, DOWN) + dot(k, sl, DOWN)
        ab_ref[h, w, :, :DK] = final * eye - moved[:, :DK]
        ab_ref[h, w, :, DK:] = moved[:, DK:]


def kernel(
    total, sections,
    q_ref, k_ref, v_ref, ccol_ref, crow_ref, b_ref, gain_ref, out_ref, last_ref,
    ab, recv, o_ref, p_ref, sin, sout, ent, st, fin,
    map_send, map_recv, chain_send, chain_recv, ret_send, ret_recv, fin_send, fin_recv,
):
    plane = q_ref.shape[1] // DK
    planes = sections // plane
    kept = ab.shape[1]
    rows = fin.shape[0]
    place = lax.axis_index("sec")
    z, r = place // plane, place % plane
    base = z * plane
    owner = (planes - 1) * plane + place // planes

    def remote(src, dst, send, receive, target):
        return pltpu.make_async_remote_copy(
            src_ref=src, dst_ref=dst, send_sem=send, recv_sem=receive,
            device_id={"sec": target}, device_id_type=pl.DeviceIdType.MESH,
        )

    def greet(target):
        pl.semaphore_signal(
            barrier, inc=1, device_id={"sec": target}, device_id_type=pl.DeviceIdType.MESH
        )

    barrier = pltpu.get_barrier_semaphore()
    for i in range(1, plane):
        greet(base + (r + i) % plane)
    pl.when(z > 0)(lambda: greet(place - plane))
    pl.when(owner != place)(lambda: greet(owner))
    at_end = z == planes - 1
    holders = planes - jnp.where(owner == place, 1, 0)
    expected = plane - 1 + jnp.where(at_end, holders, 1)

    def send_map(h):
        return remote(ab.at[h], recv.at[r], map_send.at[h], map_recv.at[r], base + h)

    def one_head(i, carry):
        h = (r + 1 + i) % plane
        section_map(total, h, q_ref, k_ref, v_ref, ccol_ref, crow_ref, b_ref, ab, o_ref, p_ref)
        pl.when(i == 0)(lambda: pl.semaphore_wait(barrier, expected))
        pl.when(i < plane - 1)(lambda: send_map(h).start())
        return carry

    lax.fori_loop(0, plane, one_head, 0)
    recv[r] = ab[r]

    for s in range(plane):

        @pl.when(r != s)
        def _(s=s):
            remote(ab.at[s], recv.at[s], map_send.at[s], map_recv.at[s], base + s).wait_recv()

        if s > 0:
            for e in range(kept):
                later = recv[s, e, :, :DK]
                new = dot3(later, recv[s - 1, e])
                recv[s, e, :, :DK] = new[:, :DK]
                recv[s, e, :, DK:] = new[:, DK:] + recv[s, e, :, DK:]

    def chain(e, target):
        return remote(
            sout.at[pl.ds(e * DK, DK)], sin.at[e], chain_send.at[e], chain_recv.at[e], target
        )

    @pl.when(z == 0)
    def _():
        sin[...] = jnp.zeros_like(sin)

    for e in range(kept):

        @pl.when(z > 0)
        def _(e=e):
            chain(e, place - plane).wait_recv()

        sout[e * DK : (e + 1) * DK] = (
            dot3(recv[plane - 1, e, :, :DK], sin[e]) + recv[plane - 1, e, :, DK:]
        )

        @pl.when(z < planes - 1)
        def _(e=e):
            chain(e, place + plane).start()

    def back(s):
        return remote(ent.at[s], st.at[r], ret_send.at[s], ret_recv.at[r], base + s)

    for s in range(plane):
        for e in range(kept):
            if s == 0:
                ent[s, e] = sin[e]
            else:
                ent[s, e] = dot3(recv[s - 1, e, :, :DK], sin[e]) + recv[s - 1, e, :, DK:]
        pl.when(r != s)(lambda s=s: back(s).start())
    st[r] = ent[r]

    def last_rows(c):
        return remote(
            sout.at[pl.ds(c * rows, rows)], fin, fin_send.at[c], fin_recv, r * planes + c
        )

    for c in range(planes):
        pl.when(at_end & (r * planes + c != place))(lambda c=c: last_rows(c).start())

        @pl.when(at_end & (r * planes + c == place))
        def _(c=c):
            fin[...] = sout[c * rows : (c + 1) * rows]

    def read_out(i, carry):
        h = (r + i) % plane

        @pl.when(i > 0)
        def _():
            remote(ent.at[h], st.at[h], ret_send.at[h], ret_recv.at[h], base + h).wait_recv()

        for w in range(kept):
            o = o_ref[h, w] + dot3(p_ref[h, w], st[h, w])
            scale = lax.rsqrt(jnp.mean(o * o, axis=1, keepdims=True) + 1e-06)
            columns = pl.ds(pl.multiple_of((h * kept + w) * DK, DK), DK)
            out_ref[:, columns] = (o * scale * gain_ref[...]).astype(BF16)
        return carry

    lax.fori_loop(0, plane, read_out, 0)

    @pl.when(owner != place)
    def _():
        remote(sout.at[pl.ds(0, rows)], fin, fin_send.at[0], fin_recv, owner).wait_recv()

    last_ref[...] = fin[...]

    for s in range(plane):

        @pl.when(r != s)
        def _(s=s):
            send_map(s).wait_send()
            back(s).wait_send()

    for e in range(kept):
        pl.when(z < planes - 1)(lambda e=e: chain(e, place + plane).wait_send())
    for c in range(planes):
        pl.when(at_end & (r * planes + c != place))(lambda c=c: last_rows(c).wait_send())


def shards(queries, keys, values, gate_codes, beta_codes, norm_gain):
    tokens, heads = gate_codes.shape
    sections = lax.axis_size("sec")
    total = tokens * sections
    plane = queries.shape[1] // DK
    planes = sections // plane
    kept = heads // plane
    rows = heads * DK // sections
    sums = jnp.cumsum(gate_codes, axis=0).astype(F32).reshape(tokens, plane, kept)
    beta = (beta_codes.astype(F32) / total).reshape(tokens, plane, kept)
    vmem = pl.BlockSpec(memory_space=pltpu.VMEM)
    dma = pltpu.SemaphoreType.DMA
    return pl.pallas_call(
        functools.partial(kernel, total, sections),
        in_specs=[vmem] * 7,
        out_specs=[vmem] * 2,
        out_shape=[
            jax.ShapeDtypeStruct((tokens, heads * DK), BF16),
            jax.ShapeDtypeStruct((rows, DK), F32),
        ],
        scratch_shapes=[
            pltpu.VMEM((plane, kept, DK, 2 * DK), F32),
            pltpu.VMEM((plane, kept, DK, 2 * DK), F32),
            pltpu.VMEM((plane, kept, tokens, DK), F32),
            pltpu.VMEM((plane, kept, tokens, DK), F32),
            pltpu.VMEM((kept, DK, DK), F32),
            pltpu.VMEM((kept * DK, DK), F32),
            pltpu.VMEM((plane, kept, DK, DK), F32),
            pltpu.VMEM((plane, kept, DK, DK), F32),
            pltpu.VMEM((rows, DK), F32),
            dma((plane,)), dma((plane,)), dma((kept,)), dma((kept,)),
            dma((plane,)), dma((plane,)), dma((planes,)), dma,
        ],
        compiler_params=pltpu.CompilerParams(
            vmem_limit_bytes=48 * 1024 * 1024, collective_id=0, has_side_effects=True
        ),
        name="recurrence",
    )(
        queries,
        keys,
        values,
        jnp.transpose(sums, (1, 0, 2)),
        jnp.transpose(sums, (1, 2, 0)),
        jnp.transpose(beta, (1, 0, 2)),
        norm_gain.reshape(1, DK),
    )


def solution(mesh):
    rows = P(("parts", "sec"), None)
    return jax.shard_map(
        shards,
        mesh=mesh,
        in_specs=(rows, rows, rows, rows, rows, P()),
        out_specs=(rows, rows),
        check_vma=False,
    )
```

```python
import functools

import jax
import jax.numpy as jnp
from jax import lax
from jax.experimental import pallas as pl
from jax.experimental.pallas import tpu as pltpu
from jax.sharding import PartitionSpec as P

DK = 128
HALF = 128
F32 = jnp.float32
BF16 = jnp.bfloat16
ROWS_BY_ROWS = (((1,), (1,)), ((), ()))
DOWN = (((0,), (0,)), ((), ()))
PLAIN = (((1,), (0,)), ((), ()))


def cut(a):
    high = a.astype(BF16)
    return high, (a - high.astype(F32)).astype(BF16)


def dot(left, right, dims=PLAIN):
    return lax.dot_general(left, right, dims, preferred_element_type=F32)


def product(left, right):
    (lh, ll), (rh, rl) = left, right
    if lh.shape[1] > DK:
        return dot(lh, rh) + (dot(lh, rl) + dot(ll, rh))
    wide = jnp.concatenate([lh, ll], axis=1)
    if rh.shape[1] > DK:
        return dot(wide, jnp.concatenate([rh, rh], axis=0)) + dot(lh, rl)
    both = jnp.concatenate([rh, rl], axis=1)
    halves = dot(wide, jnp.concatenate([both, both], axis=0))
    return halves[:, :DK] + halves[:, DK:]


def dot3(left, right):
    return product(cut(left), cut(right))


def section_map(total, h, q_ref, k_ref, v_ref, ccol_ref, crow_ref, b_ref, ab_ref, o_ref, p_ref):
    tokens = q_ref.shape[0]
    key_heads = q_ref.shape[1] // DK
    group = v_ref.shape[1] // DK // key_heads
    q = q_ref[:, pl.ds(pl.multiple_of(h * DK, DK), DK)]
    k = k_ref[:, pl.ds(pl.multiple_of(h * DK, DK), DK)]
    v = v_ref[:, pl.ds(pl.multiple_of(h * group * DK, DK), group * DK)]
    ccols, crows, betas = ccol_ref[h], crow_ref[h], b_ref[h]
    qf = q.astype(F32)
    kf = k.astype(F32)
    rq = lax.rsqrt(jnp.sum(qf * qf, axis=1, keepdims=True) + 1e-06) * DK ** (-0.5)
    rk = lax.rsqrt(jnp.sum(kf * kf, axis=1, keepdims=True) + 1e-06)
    rk_row = jnp.transpose(jnp.broadcast_to(rk, (tokens, DK)))[0:1, :]
    kk = dot(k, k, ROWS_BY_ROWS) * rk * rk_row
    qk = dot(q, k, ROWS_BY_ROWS) * rq * rk_row
    row = lax.broadcasted_iota(jnp.int32, (tokens, tokens), 0)
    col = lax.broadcasted_iota(jnp.int32, (tokens, tokens), 1)
    r = row[:HALF, :HALF]
    c = col[:HALF, :HALF]
    eye = (r == c).astype(F32)
    blocks = tokens // HALF
    lowers, xs, data = [], [], []
    for w in range(group):
        ccol = ccols[:, w : w + 1]
        crow = crows[w : w + 1, :]
        beta = betas[:, w : w + 1]
        gap = jnp.where(row >= col, (ccol - crow) * (-1.0 / total), -1e30)
        mask = jnp.exp(gap)
        lower = jnp.where(row > col, kk * mask * beta, 0.0)
        grown = jnp.exp(ccol * (-1.0 / total))
        last = ccol[tokens - 1 : tokens, :]
        left = jnp.exp((last - ccol) * (-1.0 / total)) * rk
        final = jnp.exp(last * (-1.0 / total))
        right = jnp.concatenate(
            [kf * (rk * beta * grown), v[:, w * DK : (w + 1) * DK].astype(F32) * beta], axis=1
        )
        data.append((lower, qk * mask, grown, left, final, right))
        for b in range(blocks):
            part = lower[b * HALF : (b + 1) * HALF, b * HALF : (b + 1) * HALF]
            lowers.append(part)
    near = (r >> 4) == (c >> 4)
    ns = [jnp.where(near, part, 0.0) for part in lowers]
    seconds = [product(x, x) for x in map(cut, ns)]
    cuts = [cut(x) for x in seconds]
    both = [product(cut(jnp.concatenate([n, f], axis=0)), x) for n, f, x in zip(ns, seconds, cuts)]
    xs = [eye - n + f - g[:HALF] for n, f, g in zip(ns, seconds, both)]
    cuts = [cut(g[HALF:]) for g in both]
    both = [
        product(cut(jnp.concatenate([x, g[HALF:]], axis=0)), y) for x, g, y in zip(xs, both, cuts)
    ]
    xs = [x + g[:HALF] for x, g in zip(xs, both)]
    xs = [x + product(cut(x), cut(g[HALF:])) for x, g in zip(xs, both)]
    bit = 4
    while (1 << bit) < HALF:
        inside = ((r >> (bit + 1)) == (c >> (bit + 1))) & ((r >> bit) != (c >> bit))
        cuts = [cut(x) for x in xs]
        mids = [product(cut(jnp.where(inside, part, 0.0)), x) for part, x in zip(lowers, cuts)]
        xs = [x - product(y, cut(mid)) for x, y, mid in zip(xs, cuts, mids)]
        bit += 1
    for w in range(group):
        lower, scores, grown, left, final, right = data[w]
        parts = []
        for b in range(blocks):
            rows = slice(b * HALF, (b + 1) * HALF)
            rhs = right[rows]
            for e in range(b):
                rhs = rhs - dot3(lower[rows, e * HALF : (e + 1) * HALF], parts[e])
            parts.append(dot3(xs[w * blocks + b], rhs))
        solved = jnp.concatenate(parts, axis=0)
        read = dot3(scores, solved)
        o_ref[h, w] = read[:, DK:]
        p_ref[h, w] = qf * (rq * grown) - read[:, :DK]
        sh, sl = cut(solved * left)
        moved = dot(k, sh, DOWN) + dot(k, sl, DOWN)
        ab_ref[h, w, :, :DK] = final * eye - moved[:, :DK]
        ab_ref[h, w, :, DK:] = moved[:, DK:]


def kernel(
    total, sections,
    q_hbm, k_hbm, v_hbm, codes_ref, betas_ref, gain_ref, out_ref, last_ref,
    q_ref, k_ref, v_ref, ccol_ref, crow_ref, b_ref, in_sem,
    ab, recv, o_ref, p_ref, sin, sout, ent, st, fin,
    map_send, map_recv, chain_send, chain_recv, ret_send, ret_recv, fin_send, fin_recv,
):
    plane = q_ref.shape[1] // DK
    planes = sections // plane
    kept = ab.shape[1]
    rows = fin.shape[0]
    place = lax.axis_index("sec")
    z, r = place // plane, place % plane
    base = z * plane
    owner = (planes - 1) * plane + place // planes

    def remote(src, dst, send, receive, target):
        return pltpu.make_async_remote_copy(
            src_ref=src, dst_ref=dst, send_sem=send, recv_sem=receive,
            device_id={"sec": target}, device_id_type=pl.DeviceIdType.MESH,
        )

    def greet(target):
        pl.semaphore_signal(
            barrier, inc=1, device_id={"sec": target}, device_id_type=pl.DeviceIdType.MESH
        )

    copies = [
        pltpu.make_async_copy(src, dst, in_sem.at[i])
        for i, (src, dst) in enumerate(((q_hbm, q_ref), (k_hbm, k_ref), (v_hbm, v_ref)))
    ]
    for copy in copies:
        copy.start()
    barrier = pltpu.get_barrier_semaphore()
    for i in range(1, plane):
        greet(base + (r + i) % plane)
    pl.when(z > 0)(lambda: greet(place - plane))
    pl.when(owner != place)(lambda: greet(owner))
    at_end = z == planes - 1
    holders = planes - jnp.where(owner == place, 1, 0)
    expected = plane - 1 + jnp.where(at_end, holders, 1)

    tokens = codes_ref.shape[0]
    row = lax.broadcasted_iota(jnp.int32, (tokens, tokens), 0)
    col = lax.broadcasted_iota(jnp.int32, (tokens, tokens), 1)
    until = (row >= col).astype(F32).astype(BF16)
    codes = codes_ref[...]
    high = (codes >> 7).astype(F32).astype(BF16)
    low = (codes & 127).astype(F32).astype(BF16)
    cols = dot(until, high) * 128.0 + dot(until, low)
    across = (((0,), (1,)), ((), ()))
    crows = dot(high, until, across) * 128.0 + dot(low, until, across)
    betas = betas_ref[...].astype(F32) * (1.0 / total)
    for j in range(plane):
        ccol_ref[j] = cols[:, j * kept : (j + 1) * kept]
        crow_ref[j] = crows[j * kept : (j + 1) * kept]
        b_ref[j] = betas[:, j * kept : (j + 1) * kept]
    for copy in copies:
        copy.wait()

    def send_map(h):
        return remote(ab.at[h], recv.at[r], map_send.at[h], map_recv.at[r], base + h)

    def one_head(i, carry):
        h = (r + 1 + i) % plane
        section_map(total, h, q_ref, k_ref, v_ref, ccol_ref, crow_ref, b_ref, ab, o_ref, p_ref)
        pl.when(i == 0)(lambda: pl.semaphore_wait(barrier, expected))
        pl.when(i < plane - 1)(lambda: send_map(h).start())
        return carry

    lax.fori_loop(0, plane, one_head, 0)
    recv[r] = ab[r]

    for s in range(plane):

        @pl.when(r != s)
        def _(s=s):
            remote(ab.at[s], recv.at[s], map_send.at[s], map_recv.at[s], base + s).wait_recv()

        if s > 0:
            for e in range(kept):
                later = recv[s, e, :, :DK]
                new = dot3(later, recv[s - 1, e])
                recv[s, e, :, :DK] = new[:, :DK]
                recv[s, e, :, DK:] = new[:, DK:] + recv[s, e, :, DK:]

    def chain(e, target):
        return remote(
            sout.at[pl.ds(e * DK, DK)], sin.at[e], chain_send.at[e], chain_recv.at[e], target
        )

    @pl.when(z == 0)
    def _():
        sin[...] = jnp.zeros_like(sin)

    for e in range(kept):

        @pl.when(z > 0)
        def _(e=e):
            chain(e, place - plane).wait_recv()

        sout[e * DK : (e + 1) * DK] = (
            dot3(recv[plane - 1, e, :, :DK], sin[e]) + recv[plane - 1, e, :, DK:]
        )

        @pl.when(z < planes - 1)
        def _(e=e):
            chain(e, place + plane).start()

    def back(s):
        return remote(ent.at[s], st.at[r], ret_send.at[s], ret_recv.at[r], base + s)

    for s in range(plane):
        for e in range(kept):
            if s == 0:
                ent[s, e] = sin[e]
            else:
                ent[s, e] = dot3(recv[s - 1, e, :, :DK], sin[e]) + recv[s - 1, e, :, DK:]
        pl.when(r != s)(lambda s=s: back(s).start())
    st[r] = ent[r]

    def last_rows(c):
        return remote(
            sout.at[pl.ds(c * rows, rows)], fin, fin_send.at[c], fin_recv, r * planes + c
        )

    for c in range(planes):
        pl.when(at_end & (r * planes + c != place))(lambda c=c: last_rows(c).start())

        @pl.when(at_end & (r * planes + c == place))
        def _(c=c):
            fin[...] = sout[c * rows : (c + 1) * rows]

    def read_out(i, carry):
        h = (r + i) % plane

        @pl.when(i > 0)
        def _():
            remote(ent.at[h], st.at[h], ret_send.at[h], ret_recv.at[h], base + h).wait_recv()

        for w in range(kept):
            o = o_ref[h, w] + dot3(p_ref[h, w], st[h, w])
            scale = lax.rsqrt(jnp.mean(o * o, axis=1, keepdims=True) + 1e-06)
            columns = pl.ds(pl.multiple_of((h * kept + w) * DK, DK), DK)
            out_ref[:, columns] = (o * scale * gain_ref[...]).astype(BF16)
        return carry

    lax.fori_loop(0, plane, read_out, 0)

    @pl.when(owner != place)
    def _():
        remote(sout.at[pl.ds(0, rows)], fin, fin_send.at[0], fin_recv, owner).wait_recv()

    last_ref[...] = fin[...]

    for s in range(plane):

        @pl.when(r != s)
        def _(s=s):
            send_map(s).wait_send()
            back(s).wait_send()

    for e in range(kept):
        pl.when(z < planes - 1)(lambda e=e: chain(e, place + plane).wait_send())
    for c in range(planes):
        pl.when(at_end & (r * planes + c != place))(lambda c=c: last_rows(c).wait_send())


def shards(queries, keys, values, gate_codes, beta_codes, norm_gain):
    tokens, heads = gate_codes.shape
    sections = lax.axis_size("sec")
    total = tokens * sections
    plane = queries.shape[1] // DK
    planes = sections // plane
    kept = heads // plane
    rows = heads * DK // sections
    vmem = pl.BlockSpec(memory_space=pltpu.VMEM)
    dma = pltpu.SemaphoreType.DMA
    return pl.pallas_call(
        functools.partial(kernel, total, sections),
        in_specs=[pl.BlockSpec(memory_space=pl.ANY)] * 3 + [vmem] * 3,
        out_specs=[vmem] * 2,
        out_shape=[
            jax.ShapeDtypeStruct((tokens, heads * DK), BF16),
            jax.ShapeDtypeStruct((rows, DK), F32),
        ],
        scratch_shapes=[
            pltpu.VMEM(queries.shape, BF16),
            pltpu.VMEM(keys.shape, BF16),
            pltpu.VMEM(values.shape, BF16),
            pltpu.VMEM((plane, tokens, kept), F32),
            pltpu.VMEM((plane, kept, tokens), F32),
            pltpu.VMEM((plane, tokens, kept), F32),
            dma((3,)),
            pltpu.VMEM((plane, kept, DK, 2 * DK), F32),
            pltpu.VMEM((plane, kept, DK, 2 * DK), F32),
            pltpu.VMEM((plane, kept, tokens, DK), F32),
            pltpu.VMEM((plane, kept, tokens, DK), F32),
            pltpu.VMEM((kept, DK, DK), F32),
            pltpu.VMEM((kept * DK, DK), F32),
            pltpu.VMEM((plane, kept, DK, DK), F32),
            pltpu.VMEM((plane, kept, DK, DK), F32),
            pltpu.VMEM((rows, DK), F32),
            dma((plane,)), dma((plane,)), dma((kept,)), dma((kept,)),
            dma((plane,)), dma((plane,)), dma((planes,)), dma,
        ],
        compiler_params=pltpu.CompilerParams(
            vmem_limit_bytes=48 * 1024 * 1024, collective_id=0, has_side_effects=True
        ),
        name="recurrence",
    )(
        queries,
        keys,
        values,
        gate_codes,
        beta_codes,
        norm_gain.reshape(1, DK),
    )


def solution(mesh):
    rows = P(("parts", "sec"), None)
    return jax.shard_map(
        shards,
        mesh=mesh,
        in_specs=(rows, rows, rows, rows, rows, P()),
        out_specs=(rows, rows),
        check_vma=False,
    )
```

```python
import functools

import jax
import jax.numpy as jnp
from jax import lax
from jax.experimental import pallas as pl
from jax.experimental.pallas import tpu as pltpu
from jax.sharding import PartitionSpec as P

DK = 128
HALF = 128
F32 = jnp.float32
BF16 = jnp.bfloat16
ROWS_BY_ROWS = (((1,), (1,)), ((), ()))
DOWN = (((0,), (0,)), ((), ()))
PLAIN = (((1,), (0,)), ((), ()))


def cut(a):
    high = a.astype(BF16)
    return high, (a - high.astype(F32)).astype(BF16)


def dot(left, right, dims=PLAIN):
    return lax.dot_general(left, right, dims, preferred_element_type=F32)


def product(left, right):
    (lh, ll), (rh, rl) = left, right
    if lh.shape[1] > DK:
        return dot(lh, rh) + (dot(lh, rl) + dot(ll, rh))
    wide = jnp.concatenate([lh, ll], axis=1)
    if rh.shape[1] > DK:
        return dot(wide, jnp.concatenate([rh, rh], axis=0)) + dot(lh, rl)
    both = jnp.concatenate([rh, rl], axis=1)
    halves = dot(wide, jnp.concatenate([both, both], axis=0))
    return halves[:, :DK] + halves[:, DK:]


def dot3(left, right):
    return product(cut(left), cut(right))


def section_map(total, hs, q_ref, k_ref, v_ref, ccol_ref, crow_ref, b_ref, ab_ref, o_ref, p_ref):
    tokens = q_ref.shape[0]
    key_heads = q_ref.shape[1] // DK
    group = v_ref.shape[1] // DK // key_heads
    row = lax.broadcasted_iota(jnp.int32, (tokens, tokens), 0)
    col = lax.broadcasted_iota(jnp.int32, (tokens, tokens), 1)
    r = row[:HALF, :HALF]
    c = col[:HALF, :HALF]
    eye = (r == c).astype(F32)
    blocks = tokens // HALF
    lowers, xs, data = [], [], []
    for h in hs:
        q = q_ref[:, pl.ds(pl.multiple_of(h * DK, DK), DK)]
        k = k_ref[:, pl.ds(pl.multiple_of(h * DK, DK), DK)]
        v = v_ref[:, pl.ds(pl.multiple_of(h * group * DK, DK), group * DK)]
        ccols, crows, betas = ccol_ref[h], crow_ref[h], b_ref[h]
        qf = q.astype(F32)
        kf = k.astype(F32)
        rq = lax.rsqrt(jnp.sum(qf * qf, axis=1, keepdims=True) + 1e-06) * DK ** (-0.5)
        rk = lax.rsqrt(jnp.sum(kf * kf, axis=1, keepdims=True) + 1e-06)
        rk_row = jnp.transpose(jnp.broadcast_to(rk, (tokens, DK)))[0:1, :]
        kk = dot(k, k, ROWS_BY_ROWS) * rk * rk_row
        qk = dot(q, k, ROWS_BY_ROWS) * rq * rk_row
        for w in range(group):
            ccol = ccols[:, w : w + 1]
            crow = crows[w : w + 1, :]
            beta = betas[:, w : w + 1]
            gap = jnp.where(row >= col, (ccol - crow) * (-1.0 / total), -1e30)
            mask = jnp.exp(gap)
            lower = jnp.where(row > col, kk * mask * beta, 0.0)
            grown = jnp.exp(ccol * (-1.0 / total))
            last = ccol[tokens - 1 : tokens, :]
            left = jnp.exp((last - ccol) * (-1.0 / total)) * rk
            final = jnp.exp(last * (-1.0 / total))
            right = jnp.concatenate(
                [kf * (rk * beta * grown), v[:, w * DK : (w + 1) * DK].astype(F32) * beta], axis=1
            )
            data.append((h, w, k, qf * (rq * grown), lower, qk * mask, left, final, right))
            for b in range(blocks):
                part = lower[b * HALF : (b + 1) * HALF, b * HALF : (b + 1) * HALF]
                lowers.append(part)
    near = (r >> 4) == (c >> 4)
    ns = [jnp.where(near, part, 0.0) for part in lowers]
    seconds = [product(x, x) for x in map(cut, ns)]
    cuts = [cut(x) for x in seconds]
    both = [product(cut(jnp.concatenate([n, f], axis=0)), x) for n, f, x in zip(ns, seconds, cuts)]
    xs = [eye - n + f - g[:HALF] for n, f, g in zip(ns, seconds, both)]
    cuts = [cut(g[HALF:]) for g in both]
    both = [
        product(cut(jnp.concatenate([x, g[HALF:]], axis=0)), y) for x, g, y in zip(xs, both, cuts)
    ]
    xs = [x + g[:HALF] for x, g in zip(xs, both)]
    xs = [x + product(cut(x), cut(g[HALF:])) for x, g in zip(xs, both)]
    bit = 4
    while (1 << bit) < HALF:
        inside = ((r >> (bit + 1)) == (c >> (bit + 1))) & ((r >> bit) != (c >> bit))
        cuts = [cut(x) for x in xs]
        mids = [product(cut(jnp.where(inside, part, 0.0)), x) for part, x in zip(lowers, cuts)]
        xs = [x - product(y, cut(mid)) for x, y, mid in zip(xs, cuts, mids)]
        bit += 1
    for n, (h, w, k, reach, lower, scores, left, final, right) in enumerate(data):
        parts = []
        for b in range(blocks):
            rows = slice(b * HALF, (b + 1) * HALF)
            rhs = right[rows]
            for e in range(b):
                rhs = rhs - dot3(lower[rows, e * HALF : (e + 1) * HALF], parts[e])
            parts.append(dot3(xs[n * blocks + b], rhs))
        solved = jnp.concatenate(parts, axis=0)
        read = dot3(scores, solved)
        o_ref[h, w] = read[:, DK:]
        p_ref[h, w] = reach - read[:, :DK]
        sh, sl = cut(solved * left)
        moved = dot(k, sh, DOWN) + dot(k, sl, DOWN)
        ab_ref[h, w, :, :DK] = final * eye - moved[:, :DK]
        ab_ref[h, w, :, DK:] = moved[:, DK:]


def kernel(
    total, sections,
    q_hbm, k_hbm, v_hbm, codes_ref, betas_ref, gain_ref, out_ref, last_ref,
    q_ref, k_ref, v_ref, ccol_ref, crow_ref, b_ref, in_sem,
    ab, recv, o_ref, p_ref, sin, sout, ent, st, fin,
    map_send, map_recv, chain_send, chain_recv, ret_send, ret_recv, fin_send, fin_recv,
):
    plane = q_ref.shape[1] // DK
    planes = sections // plane
    kept = ab.shape[1]
    rows = fin.shape[0]
    place = lax.axis_index("sec")
    z, r = place // plane, place % plane
    base = z * plane
    owner = (planes - 1) * plane + place // planes

    def remote(src, dst, send, receive, target):
        return pltpu.make_async_remote_copy(
            src_ref=src, dst_ref=dst, send_sem=send, recv_sem=receive,
            device_id={"sec": target}, device_id_type=pl.DeviceIdType.MESH,
        )

    def greet(target):
        pl.semaphore_signal(
            barrier, inc=1, device_id={"sec": target}, device_id_type=pl.DeviceIdType.MESH
        )

    copies = [
        pltpu.make_async_copy(src, dst, in_sem.at[i])
        for i, (src, dst) in enumerate(((q_hbm, q_ref), (k_hbm, k_ref), (v_hbm, v_ref)))
    ]
    for copy in copies:
        copy.start()
    barrier = pltpu.get_barrier_semaphore()
    for i in range(1, plane):
        greet(base + (r + i) % plane)
    pl.when(z > 0)(lambda: greet(place - plane))
    pl.when(owner != place)(lambda: greet(owner))
    at_end = z == planes - 1
    holders = planes - jnp.where(owner == place, 1, 0)
    expected = plane - 1 + jnp.where(at_end, holders, 1)

    tokens = codes_ref.shape[0]
    row = lax.broadcasted_iota(jnp.int32, (tokens, tokens), 0)
    col = lax.broadcasted_iota(jnp.int32, (tokens, tokens), 1)
    until = (row >= col).astype(F32).astype(BF16)
    codes = codes_ref[...]
    high = (codes >> 7).astype(F32).astype(BF16)
    low = (codes & 127).astype(F32).astype(BF16)
    cols = dot(until, high) * 128.0 + dot(until, low)
    across = (((0,), (1,)), ((), ()))
    crows = dot(high, until, across) * 128.0 + dot(low, until, across)
    betas = betas_ref[...].astype(F32) * (1.0 / total)
    for j in range(plane):
        ccol_ref[j] = cols[:, j * kept : (j + 1) * kept]
        crow_ref[j] = crows[j * kept : (j + 1) * kept]
        b_ref[j] = betas[:, j * kept : (j + 1) * kept]
    for copy in copies:
        copy.wait()

    def send_map(h):
        return remote(ab.at[h], recv.at[r], map_send.at[h], map_recv.at[r], base + h)

    def two_heads(i, carry):
        one, two = (r + 1 + 2 * i) % plane, (r + 2 + 2 * i) % plane
        section_map(
            total, (one, two), q_ref, k_ref, v_ref, ccol_ref, crow_ref, b_ref, ab, o_ref, p_ref
        )
        pl.when(i == 0)(lambda: pl.semaphore_wait(barrier, expected))
        send_map(one).start()
        pl.when(i < plane // 2 - 1)(lambda: send_map(two).start())
        return carry

    lax.fori_loop(0, plane // 2, two_heads, 0)
    recv[r] = ab[r]

    for s in range(plane):

        @pl.when(r != s)
        def _(s=s):
            remote(ab.at[s], recv.at[s], map_send.at[s], map_recv.at[s], base + s).wait_recv()

        if s > 0:
            for e in range(kept):
                later = recv[s, e, :, :DK]
                new = dot3(later, recv[s - 1, e])
                recv[s, e, :, :DK] = new[:, :DK]
                recv[s, e, :, DK:] = new[:, DK:] + recv[s, e, :, DK:]

    def chain(e, target):
        return remote(
            sout.at[pl.ds(e * DK, DK)], sin.at[e], chain_send.at[e], chain_recv.at[e], target
        )

    @pl.when(z == 0)
    def _():
        sin[...] = jnp.zeros_like(sin)

    for e in range(kept):

        @pl.when(z > 0)
        def _(e=e):
            chain(e, place - plane).wait_recv()

        sout[e * DK : (e + 1) * DK] = (
            dot3(recv[plane - 1, e, :, :DK], sin[e]) + recv[plane - 1, e, :, DK:]
        )

        @pl.when(z < planes - 1)
        def _(e=e):
            chain(e, place + plane).start()

    def back(s):
        return remote(ent.at[s], st.at[r], ret_send.at[s], ret_recv.at[r], base + s)

    for s in range(plane):
        for e in range(kept):
            if s == 0:
                ent[s, e] = sin[e]
            else:
                ent[s, e] = dot3(recv[s - 1, e, :, :DK], sin[e]) + recv[s - 1, e, :, DK:]
        pl.when(r != s)(lambda s=s: back(s).start())
    st[r] = ent[r]

    def last_rows(c):
        return remote(
            sout.at[pl.ds(c * rows, rows)], fin, fin_send.at[c], fin_recv, r * planes + c
        )

    for c in range(planes):
        pl.when(at_end & (r * planes + c != place))(lambda c=c: last_rows(c).start())

        @pl.when(at_end & (r * planes + c == place))
        def _(c=c):
            fin[...] = sout[c * rows : (c + 1) * rows]

    def read_out(i, carry):
        h = (r + i) % plane

        @pl.when(i > 0)
        def _():
            remote(ent.at[h], st.at[h], ret_send.at[h], ret_recv.at[h], base + h).wait_recv()

        for w in range(kept):
            o = o_ref[h, w] + dot3(p_ref[h, w], st[h, w])
            scale = lax.rsqrt(jnp.mean(o * o, axis=1, keepdims=True) + 1e-06)
            columns = pl.ds(pl.multiple_of((h * kept + w) * DK, DK), DK)
            out_ref[:, columns] = (o * scale * gain_ref[...]).astype(BF16)
        return carry

    lax.fori_loop(0, plane, read_out, 0)

    @pl.when(owner != place)
    def _():
        remote(sout.at[pl.ds(0, rows)], fin, fin_send.at[0], fin_recv, owner).wait_recv()

    last_ref[...] = fin[...]

    for s in range(plane):

        @pl.when(r != s)
        def _(s=s):
            send_map(s).wait_send()
            back(s).wait_send()

    for e in range(kept):
        pl.when(z < planes - 1)(lambda e=e: chain(e, place + plane).wait_send())
    for c in range(planes):
        pl.when(at_end & (r * planes + c != place))(lambda c=c: last_rows(c).wait_send())


def shards(queries, keys, values, gate_codes, beta_codes, norm_gain):
    tokens, heads = gate_codes.shape
    sections = lax.axis_size("sec")
    total = tokens * sections
    plane = queries.shape[1] // DK
    planes = sections // plane
    kept = heads // plane
    rows = heads * DK // sections
    vmem = pl.BlockSpec(memory_space=pltpu.VMEM)
    dma = pltpu.SemaphoreType.DMA
    return pl.pallas_call(
        functools.partial(kernel, total, sections),
        in_specs=[pl.BlockSpec(memory_space=pltpu.HBM)] * 3 + [vmem] * 3,
        out_specs=[vmem] * 2,
        out_shape=[
            jax.ShapeDtypeStruct((tokens, heads * DK), BF16),
            jax.ShapeDtypeStruct((rows, DK), F32),
        ],
        scratch_shapes=[
            pltpu.VMEM(queries.shape, BF16),
            pltpu.VMEM(keys.shape, BF16),
            pltpu.VMEM(values.shape, BF16),
            pltpu.VMEM((plane, tokens, kept), F32),
            pltpu.VMEM((plane, kept, tokens), F32),
            pltpu.VMEM((plane, tokens, kept), F32),
            dma((3,)),
            pltpu.VMEM((plane, kept, DK, 2 * DK), F32),
            pltpu.VMEM((plane, kept, DK, 2 * DK), F32),
            pltpu.VMEM((plane, kept, tokens, DK), F32),
            pltpu.VMEM((plane, kept, tokens, DK), F32),
            pltpu.VMEM((kept, DK, DK), F32),
            pltpu.VMEM((kept * DK, DK), F32),
            pltpu.VMEM((plane, kept, DK, DK), F32),
            pltpu.VMEM((plane, kept, DK, DK), F32),
            pltpu.VMEM((rows, DK), F32),
            dma((plane,)), dma((plane,)), dma((kept,)), dma((kept,)),
            dma((plane,)), dma((plane,)), dma((planes,)), dma,
        ],
        compiler_params=pltpu.CompilerParams(
            vmem_limit_bytes=48 * 1024 * 1024, collective_id=0, has_side_effects=True
        ),
        name="recurrence",
    )(
        queries,
        keys,
        values,
        gate_codes,
        beta_codes,
        norm_gain.reshape(1, DK),
    )


def solution(mesh):
    rows = P(("parts", "sec"), None)
    return jax.shard_map(
        shards,
        mesh=mesh,
        in_specs=(rows, rows, rows, rows, rows, P()),
        out_specs=(rows, rows),
        check_vma=False,
    )
```
